32 devices in a mesh: groups: 2 (over x), dp: 16 (over z, y, core).
Axes of the slice: x: 2, y: 2, z: 4, core: 2. Of those that a mesh axis runs over, the one named last changes fastest.
Arguments:
- features: bfloat16 [32768, 128], P(('groups', 'dp')), parts along dimension 0, may hold values from -6 to 6
- treatment: int32 [32768], P(('groups', 'dp')), parts along dimension 0, may hold values 0 or 1
- outcome: int32 [32768], P(('groups', 'dp')), parts along dimension 0, may hold values 0 or 1
- head: bfloat16 [2, 512], replicated, may hold values from -0.25 to 0.25
- positions: float32 [8, 128, 512], P('groups'), parts along dimension 0, may hold values from -0.5 to 0.5
- momenta: float32 [8, 128, 512], P('groups'), parts along dimension 0, may hold values from -1.8 to 1.8
- inverse_temps: float32 [8], P('groups'), parts along dimension 0, may hold values from 0.1 to 1
- step_sizes: float32 [8], P('groups'), parts along dimension 0, may hold values from 0.05 to 0.15
- accept: int32 [6], P('groups'), parts along dimension 0, may hold values 0 or 1
Outputs:
- new_positions: float32 [8, 128, 512], P('groups'), parts along dimension 0
- new_momenta: float32 [8, 128, 512], P('groups'), parts along dimension 0
- mean_nll: float32 [8], P('groups'), parts along dimension 0
The draws below stay inside these ranges and needn't reach their ends.
There are 2 independent parts, one for each index of `groups`. The reference program is written for one: setup_inputs(seed, part) draws one part's arguments, and reference() takes and returns one part's arrays. A program takes and returns all parts, laid end to end along the dimension named above; an argument that names none is the same for every part. Nothing has to cross between parts.
All inputs are finite; a program needn't handle non-finite values. No bound on the sum of `treatment` or of `outcome` on one device may be relied on, other than what follows from the above.
Results may differ from the reference program's by a relative error of at most 0.013.
Values may be sent and summed in bfloat16 or wider, within the bound.
A program may use at most 64 MiB of HBM per device.

```python
import math
import jax
import jax.numpy as jnp
from jax import lax

F = 128
H = 512
RUNGS = 4
LEAPS = 4
TOKENS = 16384


def draw_features(key, part):
    key = jax.random.fold_in(key, 11)
    first = jax.random.fold_in(key, 0)
    rows = jnp.arange(TOKENS).astype(jnp.float32)
    scale = 0.5 + rows / max(TOKENS - 1, 1)
    base = jnp.clip(jax.random.normal(first, (TOKENS, F), jnp.float32), -4.0, 4.0)
    return (base * scale[:, None]).astype(jnp.bfloat16)


def set_ends(entries, own_key, low, high):
    longest = entries.shape.index(max(entries.shape))
    spots = []
    for shift in (0, 1):
        where = [jax.random.randint(jax.random.fold_in(own_key, axis), (), 0, length) for axis, length in enumerate(entries.shape)]
        where[longest] = (where[longest] + shift) % entries.shape[longest]
        spots.append(tuple(where))
    return entries.at[spots[0]].set(low).at[spots[1]].set(high)


def centred(key, shape, spread, most, held_as=jnp.bfloat16):
    drawn = jax.random.normal(key, shape, jnp.float32) * spread
    return jnp.minimum(jnp.maximum(drawn, -most), most).astype(held_as)


def setup_inputs(seed: int = 0, part: int = 0) -> dict:
    keys = jax.random.split(jax.random.key(seed), 10)
    own_keys = jax.random.split(jax.random.fold_in(keys[9], part), 10)
    return {
        "features": draw_features(jax.random.fold_in(jax.random.fold_in(keys[9], part), 71), part),
        "treatment": set_ends((jax.random.randint(own_keys[1], (TOKENS,), 0, 2) < 1).astype(jnp.int32), jax.random.fold_in(own_keys[1], 1), 0, 1),
        "outcome": set_ends((jax.random.randint(own_keys[2], (TOKENS,), 0, 5) < 2).astype(jnp.int32), jax.random.fold_in(own_keys[2], 1), 0, 1),
        "head": centred(keys[3], (2, H), H ** -0.5, 0.25),
        "positions": centred(own_keys[4], (RUNGS, F, H), F ** -0.5, 0.5, jnp.float32),
        "momenta": centred(own_keys[5], (RUNGS, F, H), 0.3, 1.8, jnp.float32),
        "inverse_temps": jnp.clip(jnp.exp(jax.random.uniform(own_keys[6], (RUNGS,), jnp.float32, math.log(0.1), math.log(1.0))), 0.1, 1.0),
        "step_sizes": jnp.clip(jnp.exp(jax.random.uniform(own_keys[7], (RUNGS,), jnp.float32, math.log(0.05), math.log(0.15))), 0.05, 0.15),
        "accept": set_ends((jax.random.randint(own_keys[8], (RUNGS - 1,), 0, 2) < 1).astype(jnp.int32), jax.random.fold_in(own_keys[8], 1), 0, 1),
    }


def totals(features, treatment, outcome, head, theta):
    weights_bf = theta.astype(jnp.bfloat16).astype(jnp.float32)
    block = math.gcd(TOKENS, 4096)
    count = TOKENS // block
    feats = features.reshape(count, block, F)
    treats = treatment.reshape(count, block)
    outs = outcome.reshape(count, block)
    head_f = head.astype(jnp.float32)

    def step(carry, item):
        grad, loss = carry
        xb, tb, yb = item
        xf = xb.astype(jnp.float32)
        pre = jnp.einsum("nf,rfh->rnh", xf, weights_bf)
        hidden = jnp.tanh(pre)
        coef = head_f[0][None, :] + tb.astype(jnp.float32)[:, None] * head_f[1][None, :]
        logit = jnp.sum(hidden * coef[None], axis=2)
        yf = yb.astype(jnp.float32)[None, :]
        nll = jax.nn.softplus(logit) - yf * logit
        resid = jax.nn.sigmoid(logit) - yf
        delta = (resid[:, :, None] * coef[None] * (1.0 - hidden * hidden)).astype(jnp.bfloat16)
        grad = grad + jnp.einsum("nf,rnh->rfh", xf, delta.astype(jnp.float32))
        loss = loss + jnp.sum(nll, axis=1)
        return (grad, loss), None

    start = (jnp.zeros((RUNGS, F, H), jnp.float32), jnp.zeros((RUNGS,), jnp.float32))
    (grad, loss), _ = lax.scan(step, start, (feats, treats, outs))
    return grad, loss


def reference(features, treatment, outcome, head, positions, momenta, inverse_temps, step_sizes, accept):
    beta = inverse_temps[:, None, None]
    eps = step_sizes[:, None, None]
    theta = positions
    moment = momenta
    grad, loss = totals(features, treatment, outcome, head, theta)
    force = beta * grad + theta
    for leap in range(LEAPS):
        moment = moment - 0.5 * eps * force
        theta = theta + eps * moment
        grad, loss = totals(features, treatment, outcome, head, theta)
        force = beta * grad + theta
        moment = moment - 0.5 * eps * force
    mean_rung = loss / TOKENS
    order = jnp.arange(RUNGS, dtype=jnp.int32)
    for k in range(RUNGS - 1):
        taken = accept[k] == 1
        lower = order[k]
        upper = order[k + 1]
        order = order.at[k].set(jnp.where(taken, upper, lower))
        order = order.at[k + 1].set(jnp.where(taken, lower, upper))
    return jnp.take(theta, order, axis=0), jnp.take(moment, order, axis=0), jnp.take(mean_rung, order, axis=0)
```

```python
import functools
import jax
import jax.numpy as jnp
from jax import lax
from jax.experimental import pallas as pl
from jax.experimental.pallas import tpu as pltpu
from jax.sharding import PartitionSpec as P

LEAPS = 4
LOCAL = 2
MESH = pl.DeviceIdType.MESH
F32 = jnp.float32
BF16 = jnp.bfloat16


def chain_kernel(
    line,
    block,
    feat_ref,
    treat_ref,
    outcome_ref,
    head_ref,
    pos_ref,
    mom_ref,
    temp_ref,
    step_ref,
    th_ref,
    mo_ref,
    loss_ref,
    load_buf,
    xt,
    ty,
    coef,
    base_b,
    effect_b,
    slope,
    pre_buf,
    near_left,
    line_left,
    full_left,
    gsum,
    near_send,
    near_recv,
    line_send,
    line_recv,
    gfull,
    loss_own,
    loss_near,
    loss_line,
    load_sem,
    in_sem,
    near_sem,
    line_sem,
    aline_sem,
    anear_sem,
    lnear_sem,
    lline_sem,
    out_sem,
):
    group = lax.axis_index("groups")
    me = lax.axis_index("dp")
    core = lax.rem(me, 2)
    near = lax.rem(me // 2, 2)
    far = me // 4
    rows = feat_ref.shape[0]
    hidden = head_ref.shape[1]
    half = hidden // 2
    shard = half // line
    items = LOCAL * (LEAPS + 1)

    def device(z, y, c):
        return (group, (z * 2 + y) * 2 + c)

    core_peer = device(far, near, 1 - core)
    near_peer = device(far, 1 - near, core)
    line_peers = [lax.rem(far + d, line) for d in range(1, line)]

    def remote(src, dst, sems, where):
        return pltpu.make_async_remote_copy(
            src_ref=src,
            dst_ref=dst,
            send_sem=sems[0],
            recv_sem=sems[1],
            device_id=where,
            device_id_type=MESH,
        )

    loads = []
    for s in range(LOCAL):
        for a, src in enumerate((pos_ref, mom_ref)):
            loads.append(
                pltpu.make_async_copy(
                    src.at[core * LOCAL + s], load_buf.at[2 * s + a], load_sem.at[2 * s + a]
                )
            )
    for copy in loads:
        copy.start()

    barrier = pltpu.get_barrier_semaphore()
    pl.semaphore_signal(barrier, inc=1, device_id=core_peer, device_id_type=MESH)
    pl.semaphore_signal(barrier, inc=1, device_id=near_peer, device_id_type=MESH)
    for z in line_peers:
        pl.semaphore_signal(
            barrier, inc=1, device_id=device(z, near, core), device_id_type=MESH
        )

    xt[0] = feat_ref[...].T
    ty[0, 0:1] = treat_ref[...].astype(F32)
    ty[0, 1:2] = outcome_ref[...].astype(F32)
    ty[0, 2:8] = jnp.zeros((6, rows), F32)
    pl.semaphore_wait(barrier, line + 1)
    copy_x = remote(xt.at[0], xt.at[1], (in_sem.at[0], in_sem.at[1]), core_peer)
    copy_t = remote(ty.at[0], ty.at[1], (in_sem.at[2], in_sem.at[3]), core_peer)
    copy_x.start()
    copy_t.start()

    loss_own[...] = jnp.zeros_like(loss_own)
    near_left[...] = jnp.zeros_like(near_left)
    line_left[...] = jnp.zeros_like(line_left)
    full_left[...] = jnp.zeros_like(full_left)
    head = head_ref[...].astype(F32)
    base_b[...] = jnp.broadcast_to(head[0:1], (128, hidden)).T
    effect_b[...] = jnp.broadcast_to(head[1:2], (128, hidden)).T
    for s in range(LOCAL):
        loads[2 * s].wait()
        th_ref[core * LOCAL + s] = load_buf[2 * s].T
        loads[2 * s + 1].wait()
        mo_ref[core * LOCAL + s] = load_buf[2 * s + 1].T
    copy_t.wait()
    for part in range(2):
        for g in range(rows // 128):
            span = slice(g * 128, (g + 1) * 128)
            coef[part, :, span] = base_b[...] + ty[part, 0:1, span] * effect_b[...]
    copy_x.wait()

    def near_reduce(slot):
        return remote(
            near_send.at[slot],
            near_recv.at[slot],
            (near_sem.at[slot, 0], near_sem.at[slot, 1]),
            near_peer,
        )

    def line_reduce(slot, d):
        z = line_peers[d]
        return remote(
            line_send.at[slot, pl.ds(pl.multiple_of(z * shard, shard), shard)],
            line_recv.at[slot, d],
            (line_sem.at[slot, d, 0], line_sem.at[slot, d, 1]),
            device(z, near, core),
        )

    def line_gather(slot, d):
        mine = pl.ds(pl.multiple_of(near * half + far * shard, shard), shard)
        return remote(
            gfull.at[slot, mine],
            gfull.at[slot, mine],
            (aline_sem.at[slot, d, 0], aline_sem.at[slot, d, 1]),
            device(line_peers[d], near, core),
        )

    def near_gather(slot):
        mine = pl.ds(pl.multiple_of(near * half, half), half)
        return remote(
            gfull.at[slot, mine],
            gfull.at[slot, mine],
            (anear_sem.at[slot, 0], anear_sem.at[slot, 1]),
            near_peer,
        )

    def loss_to_near():
        return remote(loss_own, loss_near, (lnear_sem.at[0], lnear_sem.at[1]), near_peer)

    def loss_to_line(d):
        return remote(
            loss_line.at[far],
            loss_line.at[far],
            (lline_sem.at[d, 0], lline_sem.at[d, 1]),
            device(line_peers[d], near, core),
        )

    def loss_to_core():
        mine = pl.ds(pl.multiple_of(core * 8, 8), 8)
        return remote(
            loss_ref.at[mine], loss_ref.at[mine], (out_sem.at[2, 0, 0], out_sem.at[2, 0, 1]), core_peer
        )

    def result_to_core(ref, a, slot):
        rung = core * LOCAL + slot
        return remote(
            ref.at[rung], ref.at[rung], (out_sem.at[a, slot, 0], out_sem.at[a, slot, 1]), core_peer
        )

    def carry_weight(k):
        leap = k // LOCAL
        return jnp.where(leap == 1, 0.5, jnp.where(leap == LEAPS, 2.0, 1.0)).astype(F32)

    def rounded(value, left, slot, k):
        value = value + carry_weight(k) * left[slot]
        sent = value.astype(BF16)
        left[slot] = value - sent.astype(F32)
        return sent

    def evaluate(slot, part):
        weights = th_ref[core * LOCAL + slot].astype(BF16)
        total = jnp.zeros((1, 128), F32)
        step = 64
        for b in range(rows // block):
            span = slice(b * block, (b + 1) * block)
            pre = pre_buf.at[b % 2]
            pre[...] = jnp.dot(weights, xt[part, :, span], preferred_element_type=F32)
            acc = jnp.zeros((8, block), F32)
            for j in range(0, hidden, step):
                act = jnp.tanh(pre[j : j + step])
                scale = coef[part, j : j + step, span]
                term = act * scale
                acc = acc + jnp.sum(term.reshape(step // 8, 8, block), axis=0)
                pre[j : j + step] = scale - act * term
            logit = jnp.sum(acc, axis=0, keepdims=True)
            target = ty[part, 1:2, span]
            small = jnp.exp(-jnp.abs(logit))
            nll = jnp.maximum(logit, 0.0) + jnp.log(1.0 + small) - target * logit
            resid = jnp.where(logit >= 0.0, 1.0, small) / (1.0 + small) - target
            for j in range(0, hidden, step):
                slope[j : j + step, span] = (pre[j : j + step] * resid).astype(BF16)
            for g in range(block // 128):
                total = total + nll[:, g * 128 : (g + 1) * 128]
        grad = lax.dot_general(
            slope[...], xt[part], (((1,), (1,)), ((), ())), preferred_element_type=F32
        )
        row = lax.broadcasted_iota(jnp.int32, (8, 128), 0)
        total = jnp.broadcast_to(total, (8, 128))
        if part == 0:
            gsum[slot] = grad
            loss_own[...] = jnp.where(row == slot, total, loss_own[...])
        else:
            gsum[slot] = gsum[slot] + grad
            loss_own[...] = jnp.where(row == slot, total + loss_own[...], loss_own[...])

    def send_near(k, slot):
        other = pl.ds(pl.multiple_of((1 - near) * half, half), half)
        near_send[slot] = rounded(gsum[slot, other], near_left, slot, k)
        near_reduce(slot).start()

        @pl.when(k == items - 1)
        def _():
            loss_to_near().start()

    def reduced_near(k, slot):
        near_reduce(slot).wait()
        mine = pl.ds(pl.multiple_of(near * half, half), half)
        summed = gsum[slot, mine] + near_recv[slot].astype(F32)
        gsum[slot, mine] = summed
        line_send[slot] = rounded(summed, line_left, slot, k)
        for d in range(line - 1):
            line_reduce(slot, d).start()

        @pl.when(k == items - 1)
        def _():
            loss_to_near().wait()
            loss_line[far] = loss_own[...] + loss_near[...]
            for d in range(line - 1):
                loss_to_line(d).start()

    def reduced_line(k, slot):
        mine = pl.ds(pl.multiple_of(near * half + far * shard, shard), shard)
        summed = gsum[slot, mine]
        for d in range(line - 1):
            line_reduce(slot, d).wait()
            summed = summed + line_recv[slot, d].astype(F32)
        gfull[slot, mine] = rounded(summed, full_left, slot, k)
        for d in range(line - 1):
            line_gather(slot, d).start()

        @pl.when(k == items - 1)
        def _():
            for d in range(line - 1):
                loss_to_line(d).wait()
            whole = loss_line[0]
            for z in range(1, line):
                whole = whole + loss_line[z]
            loss_ref[pl.ds(pl.multiple_of(core * 8, 8), 8)] = whole
            loss_to_core().start()

    def gathered_line(slot):
        for d in range(line - 1):
            line_gather(slot, d).wait()
        near_gather(slot).start()

    def gathered_near(k, slot):
        near_gather(slot).wait()
        leap = k // LOCAL
        rung = core * LOCAL + slot
        eps = step_ref[rung]
        edge = jnp.logical_or(leap == 0, leap == LEAPS)
        kick = jnp.where(edge, 0.5 * eps, eps)
        theta = th_ref[rung]
        force = temp_ref[rung] * gfull[slot].astype(F32) + theta
        moment = mo_ref[rung] - kick * force
        mo_ref[rung] = moment

        @pl.when(leap < LEAPS)
        def _():
            th_ref[rung] = theta + eps * moment

        @pl.when(leap == LEAPS - 1)
        def _():
            result_to_core(th_ref, 0, slot).start()

        @pl.when(leap == LEAPS)
        def _():
            result_to_core(mo_ref, 1, slot).start()

    def turn(k, carry):
        slot = lax.rem(k, LOCAL)
        before = 1 - slot

        @pl.when(k < items)
        def _():
            evaluate(slot, 0)

        @pl.when(k >= 1)
        def _():
            reduced_line(k - 1, before)

        @pl.when(k < items)
        def _():
            evaluate(slot, 1)
            send_near(k, slot)

        @pl.when(k >= 1)
        def _():
            gathered_line(before)

        @pl.when(k < items)
        def _():
            reduced_near(k, slot)

        @pl.when(k >= 1)
        def _():
            gathered_near(k - 1, before)

        return carry

    lax.fori_loop(0, items + 1, turn, 0)
    for s in range(LOCAL):
        result_to_core(th_ref, 0, s).wait()
        result_to_core(mo_ref, 1, s).wait()
    loss_to_core().wait()


def swap_kernel(total_rows, rungs, th_ref, mo_ref, loss_ref, accept_ref, pos_out, mom_out, mean_out):
    order = [jnp.int32(r) for r in range(rungs)]
    for k in range(rungs - 1):
        taken = accept_ref[k] == 1
        lower, upper = order[k], order[k + 1]
        order[k] = jnp.where(taken, upper, lower)
        order[k + 1] = jnp.where(taken, lower, upper)
    means = []
    for r in range(rungs):
        row = (r // LOCAL) * 8 + r % LOCAL
        means.append(jnp.sum(loss_ref[row : row + 1, :]) / total_rows)
    for r in range(rungs):
        pos_out[r] = th_ref[order[r]].T
        mom_out[r] = mo_ref[order[r]].T
        mean = means[0]
        for s in range(1, rungs):
            mean = jnp.where(order[r] == s, means[s], mean)
        mean_out[r] = mean


def local(
    features, treatment, outcome, head, positions, momenta, inverse_temps, step_sizes, accept
):
    rungs, width, hidden = positions.shape
    rows = features.shape[0]
    devices = lax.axis_size("dp")
    line = devices // 4
    vmem = pl.BlockSpec(memory_space=pltpu.VMEM)
    smem = pl.BlockSpec(memory_space=pltpu.SMEM)
    anywhere = pl.BlockSpec(memory_space=pl.ANY)
    half = hidden // 2
    shard = half // line
    block = 256
    dma = pltpu.SemaphoreType.DMA
    theta, moment, loss = pl.pallas_call(
        functools.partial(chain_kernel, line, block),
        out_shape=(
            jax.ShapeDtypeStruct((rungs, hidden, width), F32),
            jax.ShapeDtypeStruct((rungs, hidden, width), F32),
            jax.ShapeDtypeStruct((16, 128), F32),
        ),
        in_specs=[vmem, vmem, vmem, vmem, anywhere, anywhere, smem, smem],
        out_specs=(vmem, vmem, vmem),
        scratch_shapes=[
            pltpu.VMEM((2 * LOCAL, width, hidden), F32),
            pltpu.VMEM((2, width, rows), BF16),
            pltpu.VMEM((2, 8, rows), F32),
            pltpu.VMEM((2, hidden, rows), F32),
            pltpu.VMEM((hidden, 128), F32),
            pltpu.VMEM((hidden, 128), F32),
            pltpu.VMEM((hidden, rows), BF16),
            pltpu.VMEM((2, hidden, block), F32),
            pltpu.VMEM((LOCAL, half, width), F32),
            pltpu.VMEM((LOCAL, half, width), F32),
            pltpu.VMEM((LOCAL, shard, width), F32),
            pltpu.VMEM((LOCAL, hidden, width), F32),
            pltpu.VMEM((LOCAL, half, width), BF16),
            pltpu.VMEM((LOCAL, half, width), BF16),
            pltpu.VMEM((LOCAL, half, width), BF16),
            pltpu.VMEM((LOCAL, line - 1, shard, width), BF16),
            pltpu.VMEM((LOCAL, hidden, width), BF16),
            pltpu.VMEM((8, 128), F32),
            pltpu.VMEM((8, 128), F32),
            pltpu.VMEM((line, 8, 128), F32),
            dma((2 * LOCAL,)),
            dma((4,)),
            dma((LOCAL, 2)),
            dma((LOCAL, line - 1, 2)),
            dma((LOCAL, line - 1, 2)),
            dma((LOCAL, 2)),
            dma((2,)),
            dma((line - 1, 2)),
            dma((3, LOCAL, 2)),
        ],
        compiler_params=pltpu.CompilerParams(
            collective_id=0, has_side_effects=True, vmem_limit_bytes=48 * 1024 * 1024
        ),
    )(
        features,
        treatment.reshape(1, rows),
        outcome.reshape(1, rows),
        head,
        positions,
        momenta,
        inverse_temps,
        step_sizes,
    )
    return pl.pallas_call(
        functools.partial(swap_kernel, float(rows * devices), rungs),
        out_shape=(
            jax.ShapeDtypeStruct((rungs, width, hidden), F32),
            jax.ShapeDtypeStruct((rungs, width, hidden), F32),
            jax.ShapeDtypeStruct((rungs,), F32),
        ),
        in_specs=[vmem, vmem, vmem, smem],
        out_specs=(vmem, vmem, smem),
        compiler_params=pltpu.CompilerParams(vmem_limit_bytes=32 * 1024 * 1024),
    )(theta, moment, loss, accept)


def solution(mesh):
    placed = (
        P(("groups", "dp"), None),
        P(("groups", "dp")),
        P(("groups", "dp")),
        P(),
        P("groups", None, None),
        P("groups", None, None),
        P("groups"),
        P("groups"),
        P("groups"),
    )
    return jax.shard_map(
        local,
        mesh=mesh,
        in_specs=placed,
        out_specs=(P("groups", None, None), P("groups", None, None), P("groups")),
        check_vma=False,
    )
```

```python
import functools
import jax
import jax.numpy as jnp
from jax import lax
from jax.experimental import pallas as pl
from jax.experimental.pallas import tpu as pltpu
from jax.sharding import PartitionSpec as P

LEAPS = 4
LOCAL = 2
MESH = pl.DeviceIdType.MESH
F32 = jnp.float32
BF16 = jnp.bfloat16


def chain_kernel(
    line,
    block,
    feat_ref,
    treat_ref,
    outcome_ref,
    head_ref,
    pos_ref,
    mom_ref,
    temp_ref,
    step_ref,
    th_ref,
    mo_ref,
    loss_ref,
    load_buf,
    xt,
    ty,
    coef,
    base_b,
    effect_b,
    slope,
    pre_buf,
    near_left,
    line_left,
    full_left,
    gsum,
    near_send,
    near_recv,
    line_send,
    line_recv,
    gfull,
    loss_own,
    loss_near,
    loss_line,
    load_sem,
    in_sem,
    near_sem,
    line_sem,
    aline_sem,
    anear_sem,
    lnear_sem,
    lline_sem,
    out_sem,
):
    group = lax.axis_index("groups")
    me = lax.axis_index("dp")
    core = lax.rem(me, 2)
    near = lax.rem(me // 2, 2)
    far = me // 4
    rows = feat_ref.shape[0]
    hidden = head_ref.shape[1]
    half = hidden // 2
    shard = half // line
    items = LOCAL * (LEAPS + 1)

    def device(z, y, c):
        return (group, (z * 2 + y) * 2 + c)

    core_peer = device(far, near, 1 - core)
    near_peer = device(far, 1 - near, core)
    line_peers = [lax.rem(far + d, line) for d in range(1, line)]

    def remote(src, dst, sems, where):
        return pltpu.make_async_remote_copy(
            src_ref=src,
            dst_ref=dst,
            send_sem=sems[0],
            recv_sem=sems[1],
            device_id=where,
            device_id_type=MESH,
        )

    loads = []
    for s in range(LOCAL):
        for a, src in enumerate((pos_ref, mom_ref)):
            loads.append(
                pltpu.make_async_copy(
                    src.at[core * LOCAL + s], load_buf.at[2 * s + a], load_sem.at[2 * s + a]
                )
            )
    for copy in loads:
        copy.start()

    barrier = pltpu.get_barrier_semaphore()
    pl.semaphore_signal(barrier, inc=1, device_id=core_peer, device_id_type=MESH)
    pl.semaphore_signal(barrier, inc=1, device_id=near_peer, device_id_type=MESH)
    for z in line_peers:
        pl.semaphore_signal(
            barrier, inc=1, device_id=device(z, near, core), device_id_type=MESH
        )

    xt[0] = feat_ref[...].T
    ty[0, 0:1] = treat_ref[...].astype(F32)
    ty[0, 1:2] = outcome_ref[...].astype(F32)
    ty[0, 2:8] = jnp.zeros((6, rows), F32)
    pl.semaphore_wait(barrier, line + 1)
    copy_x = remote(xt.at[0], xt.at[1], (in_sem.at[0], in_sem.at[1]), core_peer)
    copy_t = remote(ty.at[0], ty.at[1], (in_sem.at[2], in_sem.at[3]), core_peer)
    copy_x.start()
    copy_t.start()

    loss_own[...] = jnp.zeros_like(loss_own)
    near_left[...] = jnp.zeros_like(near_left)
    line_left[...] = jnp.zeros_like(line_left)
    full_left[...] = jnp.zeros_like(full_left)
    head = head_ref[...].astype(F32)
    base_b[...] = jnp.broadcast_to(head[0:1], (128, hidden)).T
    effect_b[...] = jnp.broadcast_to(head[1:2], (128, hidden)).T
    for s in range(LOCAL):
        loads[2 * s].wait()
        th_ref[core * LOCAL + s] = load_buf[2 * s].T
        loads[2 * s + 1].wait()
        mo_ref[core * LOCAL + s] = load_buf[2 * s + 1].T
    copy_t.wait()
    for part in range(2):
        for g in range(rows // 128):
            span = slice(g * 128, (g + 1) * 128)
            coef[part, :, span] = base_b[...] + ty[part, 0:1, span] * effect_b[...]
    copy_x.wait()

    turns = line_peers + [far]

    def near_reduce(slot, d):
        piece = pl.ds(pl.multiple_of(turns[d] * shard, shard), shard)
        return remote(
            near_send.at[slot, piece],
            near_recv.at[slot, piece],
            (near_sem.at[slot, d, 0], near_sem.at[slot, d, 1]),
            near_peer,
        )

    def line_reduce(slot, d):
        z = line_peers[d]
        return remote(
            line_send.at[slot, pl.ds(pl.multiple_of(z * shard, shard), shard)],
            line_recv.at[slot, d],
            (line_sem.at[slot, d, 0], line_sem.at[slot, d, 1]),
            device(z, near, core),
        )

    def line_gather(slot, d):
        mine = pl.ds(pl.multiple_of(near * half + far * shard, shard), shard)
        return remote(
            gfull.at[slot, mine],
            gfull.at[slot, mine],
            (aline_sem.at[slot, d, 0], aline_sem.at[slot, d, 1]),
            device(line_peers[d], near, core),
        )

    def near_gather(slot, d):
        owner = lax.rem(far + line - d, line)
        mine = pl.ds(pl.multiple_of(near * half + owner * shard, shard), shard)
        return remote(
            gfull.at[slot, mine],
            gfull.at[slot, mine],
            (anear_sem.at[slot, d, 0], anear_sem.at[slot, d, 1]),
            near_peer,
        )

    def loss_to_near():
        return remote(loss_own, loss_near, (lnear_sem.at[0], lnear_sem.at[1]), near_peer)

    def loss_to_line(d):
        return remote(
            loss_line.at[far],
            loss_line.at[far],
            (lline_sem.at[d, 0], lline_sem.at[d, 1]),
            device(line_peers[d], near, core),
        )

    def loss_to_core():
        mine = pl.ds(pl.multiple_of(core * 8, 8), 8)
        return remote(
            loss_ref.at[mine], loss_ref.at[mine], (out_sem.at[2, 0, 0], out_sem.at[2, 0, 1]), core_peer
        )

    def result_to_core(ref, a, slot):
        rung = core * LOCAL + slot
        return remote(
            ref.at[rung], ref.at[rung], (out_sem.at[a, slot, 0], out_sem.at[a, slot, 1]), core_peer
        )

    def carry_weight(k):
        leap = k // LOCAL
        return jnp.where(leap == 1, 0.5, jnp.where(leap == LEAPS, 2.0, 1.0)).astype(F32)

    def rounded(value, left, slot, k):
        value = value + carry_weight(k) * left[slot]
        sent = value.astype(BF16)
        left[slot] = value - sent.astype(F32)
        return sent

    def evaluate(slot, part):
        weights = th_ref[core * LOCAL + slot].astype(BF16)
        total = jnp.zeros((1, 128), F32)
        step = 64
        for b in range(rows // block):
            span = slice(b * block, (b + 1) * block)
            pre = pre_buf.at[b % 2]
            pre[...] = jnp.dot(weights, xt[part, :, span], preferred_element_type=F32)
            acc = jnp.zeros((8, block), F32)
            for j in range(0, hidden, step):
                act = jnp.tanh(pre[j : j + step])
                scale = coef[part, j : j + step, span]
                term = act * scale
                acc = acc + jnp.sum(term.reshape(step // 8, 8, block), axis=0)
                pre[j : j + step] = scale - act * term
            logit = jnp.sum(acc, axis=0, keepdims=True)
            target = ty[part, 1:2, span]
            small = jnp.exp(-jnp.abs(logit))
            nll = jnp.maximum(logit, 0.0) + jnp.log(1.0 + small) - target * logit
            resid = jnp.where(logit >= 0.0, 1.0, small) / (1.0 + small) - target
            for j in range(0, hidden, step):
                slope[j : j + step, span] = (pre[j : j + step] * resid).astype(BF16)
            for g in range(block // 128):
                total = total + nll[:, g * 128 : (g + 1) * 128]
        grad = lax.dot_general(
            slope[...], xt[part], (((1,), (1,)), ((), ())), preferred_element_type=F32
        )
        row = lax.broadcasted_iota(jnp.int32, (8, 128), 0)
        total = jnp.broadcast_to(total, (8, 128))
        if part == 0:
            gsum[slot] = grad
            loss_own[...] = jnp.where(row == slot, total, loss_own[...])
        else:
            gsum[slot] = gsum[slot] + grad
            loss_own[...] = jnp.where(row == slot, total + loss_own[...], loss_own[...])

    def send_near(k, slot):
        other = pl.ds(pl.multiple_of((1 - near) * half, half), half)
        near_send[slot] = rounded(gsum[slot, other], near_left, slot, k)
        for d in range(line):
            near_reduce(slot, d).start()

        @pl.when(k == items - 1)
        def _():
            loss_to_near().start()

    def reduced_near(k, slot):
        for d in range(line):
            near_reduce(slot, d).wait()
            piece = pl.ds(pl.multiple_of(turns[d] * shard, shard), shard)
            mine = pl.ds(pl.multiple_of(near * half + turns[d] * shard, shard), shard)
            summed = gsum[slot, mine] + near_recv[slot, piece].astype(F32)
            if d == line - 1:
                gsum[slot, mine] = summed
            else:
                value = summed + carry_weight(k) * line_left[slot, piece]
                sent = value.astype(BF16)
                line_left[slot, piece] = value - sent.astype(F32)
                line_send[slot, piece] = sent
                line_reduce(slot, d).start()

        @pl.when(k == items - 1)
        def _():
            loss_to_near().wait()
            loss_line[far] = loss_own[...] + loss_near[...]
            for d in range(line - 1):
                loss_to_line(d).start()

    def reduced_line(k, slot):
        mine = pl.ds(pl.multiple_of(near * half + far * shard, shard), shard)
        summed = gsum[slot, mine]
        for d in range(line - 1):
            line_reduce(slot, d).wait()
            summed = summed + line_recv[slot, d].astype(F32)
        gfull[slot, mine] = rounded(summed, full_left, slot, k)
        for d in range(line - 1):
            line_gather(slot, d).start()
        near_gather(slot, 0).start()

        @pl.when(k == items - 1)
        def _():
            for d in range(line - 1):
                loss_to_line(d).wait()
            whole = loss_line[0]
            for z in range(1, line):
                whole = whole + loss_line[z]
            loss_ref[pl.ds(pl.multiple_of(core * 8, 8), 8)] = whole
            loss_to_core().start()

    def gathered_line(slot):
        for d in range(line - 1):
            line_gather(slot, d).wait()
            near_gather(slot, d + 1).start()

    def gathered_near(k, slot):
        for d in range(line):
            near_gather(slot, d).wait()
        leap = k // LOCAL
        rung = core * LOCAL + slot
        eps = step_ref[rung]
        edge = jnp.logical_or(leap == 0, leap == LEAPS)
        kick = jnp.where(edge, 0.5 * eps, eps)
        theta = th_ref[rung]
        force = temp_ref[rung] * gfull[slot].astype(F32) + theta
        moment = mo_ref[rung] - kick * force
        mo_ref[rung] = moment

        @pl.when(leap < LEAPS)
        def _():
            th_ref[rung] = theta + eps * moment

        @pl.when(leap == LEAPS - 1)
        def _():
            result_to_core(th_ref, 0, slot).start()

        @pl.when(leap == LEAPS)
        def _():
            result_to_core(mo_ref, 1, slot).start()

    def turn(k, carry):
        slot = lax.rem(k, LOCAL)
        before = 1 - slot

        @pl.when(k < items)
        def _():
            evaluate(slot, 0)

        @pl.when(k >= 1)
        def _():
            reduced_line(k - 1, before)

        @pl.when(k < items)
        def _():
            evaluate(slot, 1)
            send_near(k, slot)

        @pl.when(k >= 1)
        def _():
            gathered_line(before)

        @pl.when(k < items)
        def _():
            reduced_near(k, slot)

        @pl.when(k >= 1)
        def _():
            gathered_near(k - 1, before)

        return carry

    lax.fori_loop(0, items + 1, turn, 0)
    for s in range(LOCAL):
        result_to_core(th_ref, 0, s).wait()
        result_to_core(mo_ref, 1, s).wait()
    loss_to_core().wait()


def swap_kernel(total_rows, rungs, th_ref, mo_ref, loss_ref, accept_ref, pos_out, mom_out, mean_out):
    order = [jnp.int32(r) for r in range(rungs)]
    for k in range(rungs - 1):
        taken = accept_ref[k] == 1
        lower, upper = order[k], order[k + 1]
        order[k] = jnp.where(taken, upper, lower)
        order[k + 1] = jnp.where(taken, lower, upper)
    means = []
    for r in range(rungs):
        row = (r // LOCAL) * 8 + r % LOCAL
        means.append(jnp.sum(loss_ref[row : row + 1, :]) / total_rows)
    for r in range(rungs):
        pos_out[r] = th_ref[order[r]].T
        mom_out[r] = mo_ref[order[r]].T
        mean = means[0]
        for s in range(1, rungs):
            mean = jnp.where(order[r] == s, means[s], mean)
        mean_out[r] = mean


def local(
    features, treatment, outcome, head, positions, momenta, inverse_temps, step_sizes, accept
):
    rungs, width, hidden = positions.shape
    rows = features.shape[0]
    devices = lax.axis_size("dp")
    line = devices // 4
    vmem = pl.BlockSpec(memory_space=pltpu.VMEM)
    smem = pl.BlockSpec(memory_space=pltpu.SMEM)
    anywhere = pl.BlockSpec(memory_space=pl.ANY)
    half = hidden // 2
    shard = half // line
    block = 256
    dma = pltpu.SemaphoreType.DMA
    theta, moment, loss = pl.pallas_call(
        functools.partial(chain_kernel, line, block),
        out_shape=(
            jax.ShapeDtypeStruct((rungs, hidden, width), F32),
            jax.ShapeDtypeStruct((rungs, hidden, width), F32),
            jax.ShapeDtypeStruct((16, 128), F32),
        ),
        in_specs=[vmem, vmem, vmem, vmem, anywhere, anywhere, smem, smem],
        out_specs=(vmem, vmem, vmem),
        scratch_shapes=[
            pltpu.VMEM((2 * LOCAL, width, hidden), F32),
            pltpu.VMEM((2, width, rows), BF16),
            pltpu.VMEM((2, 8, rows), F32),
            pltpu.VMEM((2, hidden, rows), F32),
            pltpu.VMEM((hidden, 128), F32),
            pltpu.VMEM((hidden, 128), F32),
            pltpu.VMEM((hidden, rows), BF16),
            pltpu.VMEM((2, hidden, block), F32),
            pltpu.VMEM((LOCAL, half, width), F32),
            pltpu.VMEM((LOCAL, half, width), F32),
            pltpu.VMEM((LOCAL, shard, width), F32),
            pltpu.VMEM((LOCAL, hidden, width), F32),
            pltpu.VMEM((LOCAL, half, width), BF16),
            pltpu.VMEM((LOCAL, half, width), BF16),
            pltpu.VMEM((LOCAL, half, width), BF16),
            pltpu.VMEM((LOCAL, line - 1, shard, width), BF16),
            pltpu.VMEM((LOCAL, hidden, width), BF16),
            pltpu.VMEM((8, 128), F32),
            pltpu.VMEM((8, 128), F32),
            pltpu.VMEM((line, 8, 128), F32),
            dma((2 * LOCAL,)),
            dma((4,)),
            dma((LOCAL, line, 2)),
            dma((LOCAL, line - 1, 2)),
            dma((LOCAL, line - 1, 2)),
            dma((LOCAL, line, 2)),
            dma((2,)),
            dma((line - 1, 2)),
            dma((3, LOCAL, 2)),
        ],
        compiler_params=pltpu.CompilerParams(
            collective_id=0, has_side_effects=True, vmem_limit_bytes=48 * 1024 * 1024
        ),
    )(
        features,
        treatment.reshape(1, rows),
        outcome.reshape(1, rows),
        head,
        positions,
        momenta,
        inverse_temps,
        step_sizes,
    )
    return pl.pallas_call(
        functools.partial(swap_kernel, float(rows * devices), rungs),
        out_shape=(
            jax.ShapeDtypeStruct((rungs, width, hidden), F32),
            jax.ShapeDtypeStruct((rungs, width, hidden), F32),
            jax.ShapeDtypeStruct((rungs,), F32),
        ),
        in_specs=[vmem, vmem, vmem, smem],
        out_specs=(vmem, vmem, smem),
        compiler_params=pltpu.CompilerParams(vmem_limit_bytes=32 * 1024 * 1024),
    )(theta, moment, loss, accept)


def solution(mesh):
    placed = (
        P(("groups", "dp"), None),
        P(("groups", "dp")),
        P(("groups", "dp")),
        P(),
        P("groups", None, None),
        P("groups", None, None),
        P("groups"),
        P("groups"),
        P("groups"),
    )
    return jax.shard_map(
        local,
        mesh=mesh,
        in_specs=placed,
        out_specs=(P("groups", None, None), P("groups", None, None), P("groups")),
        check_vma=False,
    )
```
